32 devices in a mesh: groups: 2 (over y), seq: 16 (over z, x, core).
Axes of the slice: x: 2, y: 2, z: 4, core: 2. Of those that a mesh axis runs over, the one named last changes fastest.
Arguments:
- hidden_now: bfloat16 [4096, 1792], P(('groups', 'seq')), parts along dimension 0, may hold values from -4 to 4
- stale_rows: bfloat16 [4096, 1792], P(('groups', 'seq')), parts along dimension 0, may hold values from -6 to 6
- expert_ids: int32 [4096, 2], P(('groups', 'seq')), parts along dimension 0, may hold values from 0 to 15, all different within a row; in each aligned block of 128 rows (0 to 127, 128 to 255, ...) at most 20 rows name the same one
- condition: float32 [3584], P('groups'), parts along dimension 0, may hold values from -5 to 5
- mod_weight: bfloat16 [1792, 5376], P(None, 'seq'), may hold values from -0.125 to 0.125
- mod_bias: float32 [5376], P('seq'), may hold values from -3 to 3
- router: bfloat16 [1792, 16], replicated, may hold values from -0.25 to 0.25
- w_gate: bfloat16 [1792, 57344], P(None, 'seq'), may hold values from -0.125 to 0.125
- w_up: bfloat16 [1792, 57344], P(None, 'seq'), may hold values from -0.125 to 0.125
- w_down: bfloat16 [57344, 1792], P('seq'), may hold values from -0.09375 to 0.09375
Outputs:
- mixed: bfloat16 [4096, 1792], P(('groups', 'seq')), parts along dimension 0
The draws below stay inside these ranges and needn't reach their ends.
There are 2 independent parts, one for each index of `groups`. The reference program is written for one: setup_inputs(seed, part) draws one part's arguments, and reference() takes and returns one part's arrays. A program takes and returns all parts, laid end to end along the dimension named above; an argument that names none is the same for every part. Nothing has to cross between parts.
Inputs may be any that keep to these rules, and one draw needn't show every extreme that they name: `expert_ids`: each token names 2 different experts. Within the 128 tokens of one aligned block no expert is named more than 20 times, and in every draw some block names some expert exactly 20 times.
All inputs are finite; a program needn't handle non-finite values.
Results may differ from the reference program's by a relative error of at most 0.0058.
Values may be sent and summed in bfloat16 or wider, within the bound.
A program may use at most 128 MiB of HBM per device.

```python
import math
import jax
import jax.numpy as jnp
import numpy as np
from jax import lax

D = 1792
FF = 3584
EXPERTS = 16
TOP = 2
TOK_DEV = 128
CAP = 20
TOKENS = 2048
GROUP = 1
N_SEQ = 16


def block_levels(own_key, shape, cuts, least, largest):
    gain = 1.0
    for position, parts in cuts:
        steps = jax.random.uniform(jax.random.fold_in(jax.random.fold_in(own_key, 6), position), (parts,), jnp.float32, least / len(cuts), largest / len(cuts))
        gain = gain * jnp.repeat(jnp.exp(steps), shape[position] // parts).reshape((-1,) + (1,) * (len(shape) - 1 - position))
    return gain


def routed_block(own_key, own, number, rows, number_of, top, limit, slope):
    ranking = jax.random.permutation(own_key, number_of)
    crowded, usual = shares(number_of, rows * top, limit, slope, True), shares(number_of, rows * top, limit, slope, False)
    places = jnp.arange(number_of)

    def named(tallies, rotation):
        used = int((tallies > 0).sum())
        fixed = max(1, used // 4)
        shifted = fixed + (places - fixed + rotation * (used - fixed)) % max(1, number_of - fixed)
        return jnp.zeros((number_of,), jnp.int32).at[ranking[jnp.where(places < fixed, places, shifted)]].set(jnp.asarray(tallies, jnp.int32))

    tallies = jnp.where(number % 4 == 0, named(crowded, number // 4), named(usual, number - number // 4 - 1))
    mixed = jax.random.permutation(jax.random.fold_in(own, 3), number_of)
    donor, taker = mixed[0:number_of // 2 * 2:2], mixed[1:number_of // 2 * 2:2]
    slack = jnp.minimum(tallies[donor] - 1, limit - tallies[taker]) // 2
    slack = jnp.where((donor == ranking[0]) | (taker == ranking[0]) | (tallies[taker] == 0), 0, jnp.maximum(slack, 0))
    shifted = jax.random.randint(jax.random.fold_in(own, 4), (number_of // 2,), 0, 1 << 20) % (slack + 1)
    tallies = tallies.at[donor].add(-shifted).at[taker].add(shifted)
    labels = jnp.searchsorted(jnp.cumsum(tallies), jnp.arange(rows * top), side="right").astype(jnp.int32)
    grid = labels.reshape(top, rows).T
    grid = grid[jax.random.permutation(jax.random.fold_in(own, 1), rows)]
    rotation = jax.random.randint(jax.random.fold_in(own, 2), (rows, 1), 0, top)
    return jnp.take_along_axis(grid, (jnp.arange(top)[None, :] + rotation) % top, axis=1)


def shares(number_of, total, bound, lean, full):
    loads = [(1 << 20) // math.isqrt(standing ** lean) + 1 for standing in range(1, number_of + 1)]
    largest = bound if full else min(bound, max(-(-total // number_of), total * loads[0] // sum(loads)))
    least = 1 if total - largest >= number_of - 1 else 0
    given, surplus = [largest] + [least] * (number_of - 1), total - largest - least * (number_of - 1)
    while surplus > 0:
        movable = [i for i in range(1, number_of) if given[i] < largest] or [i for i in range(1, number_of) if given[i] < bound]
        mass, remaining = sum([loads[i] for i in movable]), surplus
        for i in movable:
            extra = min(bound - given[i], max(1, remaining * loads[i] // mass), surplus)
            given[i] = given[i] + extra
            surplus = surplus - extra
    return np.array(given)


def bell_draw(key, shape, deviation, most, pieces=(), kind=jnp.bfloat16):
    entries = deviation * jax.random.normal(key, shape, jnp.float32)
    if pieces:
        entries = entries * block_levels(key, shape, pieces, -0.22, 0.18)
    return jnp.clip(entries, -most, most).astype(kind)


def setup_inputs(seed: int = 0, part: int = 0) -> dict:
    seeds = jax.random.split(jax.random.key(seed), 11)
    part_splits = jax.random.split(jax.random.fold_in(seeds[10], part), 11)
    hidden_now = bell_draw(part_splits[0], (TOKENS, D), 0.5, 4.0, ((0, 16),))
    stale_rows = bell_draw(part_splits[1], (TOKENS, D), 1.0, 6.0, ((0, 16),))
    expert_ids_keys = jax.random.split(jax.random.fold_in(part_splits[2], 1), TOKENS // TOK_DEV)
    expert_ids_turns = jax.random.permutation(jax.random.fold_in(part_splits[2], 3), TOKENS // TOK_DEV)
    expert_ids = jax.vmap(lambda own, number: routed_block(jax.random.fold_in(part_splits[2], 2), own, number, TOK_DEV, EXPERTS, TOP, CAP, 1))(expert_ids_keys, expert_ids_turns).reshape((TOKENS, TOP))
    condition = bell_draw(part_splits[3], (D,), 1.0, 5.0, (), jnp.float32)
    mod_weight = bell_draw(seeds[4], (D, 3 * D), D ** -0.5, 0.125, ((1, 16),))
    mod_bias = bell_draw(seeds[5], (3 * D,), 0.5, 3.0, ((0, 16),), jnp.float32)
    router = bell_draw(seeds[6], (D, EXPERTS), (D // 4) ** -0.5, 0.25)
    w_gate = bell_draw(seeds[7], (D, EXPERTS * FF), D ** -0.5, 0.125, ((1, 16),))
    w_up = bell_draw(seeds[8], (D, EXPERTS * FF), D ** -0.5, 0.125, ((1, 16),))
    w_down = bell_draw(seeds[9], (EXPERTS * FF, D), FF ** -0.5, 0.09375, ((0, 16),))
    return dict(hidden_now=hidden_now, stale_rows=stale_rows, expert_ids=expert_ids, condition=condition, mod_weight=mod_weight, mod_bias=mod_bias, router=router, w_gate=w_gate, w_up=w_up, w_down=w_down)


def token_slots(block_ids):
    flat_ids = block_ids.reshape(-1)
    expert_range = jnp.arange(EXPERTS, dtype=jnp.int32)
    onehot = (flat_ids[:, None] == expert_range[None, :]).astype(jnp.int32)
    counts = jnp.cumsum(onehot, axis=0) - 1
    return lax.optimization_barrier(jnp.sum(onehot * counts, axis=1)).reshape(block_ids.shape).astype(jnp.int32)

def reference(hidden_now, stale_rows, expert_ids, condition, mod_weight, mod_bias, router, w_gate, w_up, w_down):
    conditioned = jax.nn.silu(condition).astype(jnp.bfloat16)[None, :]
    modulation = jnp.dot(conditioned, mod_weight, preferred_element_type=jnp.float32)[0] + mod_bias
    shift_part = modulation[:D]
    scale_part = modulation[D:2 * D]
    gate_part = modulation[2 * D:]
    stream = hidden_now.astype(jnp.float32)
    row_mean = lax.optimization_barrier(jnp.mean(stream, axis=-1, keepdims=True))
    centered = stream - row_mean
    variance = lax.optimization_barrier(jnp.mean(centered * centered, axis=-1, keepdims=True))
    normed = centered * lax.rsqrt(variance + 1e-06)
    current = (normed * (1.0 + scale_part) + shift_part).astype(jnp.bfloat16)
    logits = jnp.dot(current, router, preferred_element_type=jnp.float32)
    picked = jnp.take_along_axis(logits, expert_ids, axis=1)
    weights = jax.nn.sigmoid(picked - picked[:, ::-1])
    blocks = expert_ids.reshape(N_SEQ, TOK_DEV, TOP)
    slot_index = jax.vmap(token_slots)(blocks)
    device_ids = jnp.broadcast_to(jnp.arange(N_SEQ, dtype=jnp.int32)[:, None, None], blocks.shape)
    rows_each = jnp.broadcast_to(stale_rows.reshape(N_SEQ, TOK_DEV, 1, D), (N_SEQ, TOK_DEV, TOP, D))
    buffer = jnp.zeros((N_SEQ, EXPERTS, CAP, D), jnp.bfloat16)
    buffer = buffer.at[device_ids, blocks, slot_index].set(rows_each)
    by_expert = jnp.transpose(buffer, (1, 0, 2, 3)).reshape(EXPERTS, N_SEQ * CAP, D)
    gate_all = jnp.transpose(w_gate.reshape(D, EXPERTS, FF), (1, 0, 2))
    up_all = jnp.transpose(w_up.reshape(D, EXPERTS, FF), (1, 0, 2))
    down_all = w_down.reshape(EXPERTS, FF, D)
    slice_width = FF // GROUP

    def one_expert(operands):
        expert_rows, gate_mat, up_mat, down_mat = operands
        accumulated = jnp.zeros((N_SEQ * CAP, D), jnp.float32)
        for slice_number in range(GROUP):
            first = slice_number * slice_width
            gate_val = jnp.dot(expert_rows, gate_mat[:, first:first + slice_width], preferred_element_type=jnp.float32)
            up_val = jnp.dot(expert_rows, up_mat[:, first:first + slice_width], preferred_element_type=jnp.float32)
            activation = (jax.nn.silu(gate_val) * up_val).astype(jnp.bfloat16)
            partial_out = jnp.dot(activation, down_mat[first:first + slice_width], preferred_element_type=jnp.float32)
            accumulated = accumulated + partial_out.astype(jnp.bfloat16).astype(jnp.float32)
        return accumulated
    expert_out = lax.map(one_expert, (by_expert, gate_all, up_all, down_all)).reshape(EXPERTS, N_SEQ, CAP, D)
    gathered = expert_out[blocks, device_ids, slot_index]
    routed = lax.optimization_barrier(jnp.sum(weights.reshape(N_SEQ, TOK_DEV, TOP, 1) * gathered, axis=2)).reshape(TOKENS, D)
    return (stream + gate_part * routed).astype(jnp.bfloat16)
```

```python
import functools

import jax
import jax.numpy as jnp
from jax import lax
from jax.experimental import pallas as pl
from jax.experimental.pallas import tpu as pltpu
from jax.sharding import PartitionSpec as P

EXPERTS = 16
TOP = 2
CAP = 20
BASE = 16
REST = CAP - BASE
PARTS = BASE // REST
PIECE = 512
CHUNKS = 4
MESH = pl.DeviceIdType.MESH


def pieces(width):
    return [(q, q * PIECE, min(PIECE, width - q * PIECE)) for q in range(PARTS)]


def keys_of(ids):
    rows = ids.shape[0]
    experts = lax.broadcasted_iota(jnp.int32, (rows, EXPERTS), 1)
    hot = [(ids[:, k : k + 1] == experts).astype(jnp.float32) for k in range(TOP)]
    below = (
        lax.broadcasted_iota(jnp.int32, (rows, rows), 1)
        < lax.broadcasted_iota(jnp.int32, (rows, rows), 0)
    ).astype(jnp.bfloat16)
    before = jnp.dot(
        below, (hot[0] + hot[1]).astype(jnp.bfloat16), preferred_element_type=jnp.float32
    )
    main, rest = [], []
    for k in range(TOP):
        slot = jnp.sum(hot[k] * before, axis=1, keepdims=True).astype(jnp.int32)
        first = ids[:, k : k + 1] * BASE + slot
        main.append(jnp.where(slot < BASE, first, -1))
        rest.append(jnp.where(slot >= BASE, first - BASE, -(EXPERTS + 1) * BASE))
    return hot, main, rest


def onehot(key, table):
    return (key == table).astype(jnp.float32).astype(jnp.bfloat16)


def exchange(
    n, ff_tile, d_tile, ids_ref, stale_ref, wg_hbm, wu_hbm, wd_hbm, out_ref,
    wg, wu, wd, send, recv, ret, xbuf, act,
    w_sem, out_sem, in_sem, back_sem, home_sem,
):
    width = stale_ref.shape[1]
    ff = wg.shape[1]
    group = n // EXPERTS
    half = n // 2
    per = n // CHUNKS
    me = lax.axis_index("seq")
    mine = lax.axis_index("groups")
    side, place = me // half, me % half

    loads = [
        pltpu.make_async_copy(src, dst, w_sem.at[i])
        for i, (src, dst) in enumerate(((wg_hbm, wg), (wu_hbm, wu), (wd_hbm, wd)))
    ]

    def target(k):
        far = (1 - side) * half + (place + k) % half
        near = side * half + (place + k) % half
        return jnp.where(k < half, far, near)

    def source(k):
        far = (1 - side) * half + (place + 2 * half - k) % half
        near = side * half + (place + 2 * half - k) % half
        return jnp.where(k < half, far, near)

    def rows(k):
        return pl.ds(pl.multiple_of(k * BASE, BASE), BASE)

    def outward(k):
        to = target(k)
        return pltpu.make_async_remote_copy(
            src_ref=send.at[rows(to // group)],
            dst_ref=recv.at[rows(k)],
            send_sem=out_sem.at[k],
            recv_sem=in_sem.at[k],
            device_id=(mine, to),
            device_id_type=MESH,
        )

    def homeward(k):
        return pltpu.make_async_remote_copy(
            src_ref=ret.at[rows(k)],
            dst_ref=out_ref.at[rows(me)],
            send_sem=back_sem.at[k],
            recv_sem=home_sem.at[me],
            device_id=(mine, source(k)),
            device_id_type=MESH,
        )

    barrier = pltpu.get_barrier_semaphore()

    @pl.loop(1, n)
    def _(t):
        pl.semaphore_signal(
            barrier, inc=1, device_id=(mine, (me + t) % n), device_id_type=MESH
        )

    _, main, rest = keys_of(ids_ref[...])
    stale = stale_ref[...]
    table = lax.broadcasted_iota(jnp.int32, (stale.shape[0], EXPERTS * BASE), 1)
    over_rows = (((0,), (0,)), ((), ()))
    pick = onehot(main[0], table) + onehot(main[1], table)
    send[:, :width] = lax.dot_general(
        pick, stale, over_rows, preferred_element_type=jnp.float32
    ).astype(jnp.bfloat16)
    tail = jnp.zeros((EXPERTS * BASE, PIECE), jnp.float32)
    for q, first, size in pieces(width):
        pick = onehot(rest[0] + q * REST, table) + onehot(rest[1] + q * REST, table)
        part = lax.dot_general(
            pick, stale[:, first : first + size], over_rows, preferred_element_type=jnp.float32
        )
        if size < PIECE:
            part = jnp.concatenate(
                [part, jnp.zeros((part.shape[0], PIECE - size), jnp.float32)], axis=1
            )
        tail = tail + part
    send[:, width:] = tail.astype(jnp.bfloat16)

    pl.semaphore_wait(barrier, n - 1)

    @pl.loop(0, half)
    def _(k):
        outward(k).start()

    @pl.loop(half + 1, n)
    def _(k):
        outward(k).start()

    for load in loads:
        load.start()
    recv[pl.ds(half * BASE, BASE), :] = send[rows(me // group), :]

    def work(c):
        base = c * per * BASE
        count = per * BASE
        extra = per * REST
        got = pl.ds(base, count)
        xbuf[:count] = recv[got, :width]
        across = lax.broadcasted_iota(jnp.int32, (extra, count), 1)
        down = lax.broadcasted_iota(jnp.int32, (extra, count), 0)
        spread = (down // REST) * BASE + down % REST
        tails = recv[got, width:]
        for q, first, size in pieces(width):
            xbuf[count:, first : first + size] = jnp.dot(
                onehot(spread + q * REST, across), tails[:, :size],
                preferred_element_type=jnp.float32,
            ).astype(jnp.bfloat16)
        if c == 0:
            loads[0].wait()
            loads[1].wait()

        @pl.loop(0, ff // ff_tile)
        def _(j):
            cols = pl.ds(pl.multiple_of(j * ff_tile, ff_tile), ff_tile)
            gate = jnp.dot(xbuf[...], wg[:, cols], preferred_element_type=jnp.float32)
            up = jnp.dot(xbuf[...], wu[:, cols], preferred_element_type=jnp.float32)
            act[:, cols] = (jax.nn.silu(gate) * up).astype(jnp.bfloat16)

        if c == 0:
            loads[2].wait()

        @pl.loop(0, width // d_tile)
        def _(j):
            cols = pl.ds(pl.multiple_of(j * d_tile, d_tile), d_tile)
            xbuf[:, cols] = jnp.dot(
                act[...], wd[:, cols], preferred_element_type=jnp.float32
            ).astype(jnp.bfloat16)

        ret[got, :width] = xbuf[:count]
        across = lax.broadcasted_iota(jnp.int32, (count, extra), 1)
        down = lax.broadcasted_iota(jnp.int32, (count, extra), 0)
        spread = (across // REST) * BASE + across % REST
        back = jnp.zeros((count, PIECE), jnp.float32)
        for q, first, size in pieces(width):
            part = jnp.dot(
                onehot(spread + q * REST, down), xbuf[count:, first : first + size],
                preferred_element_type=jnp.float32,
            )
            if size < PIECE:
                part = jnp.concatenate(
                    [part, jnp.zeros((count, PIECE - size), jnp.float32)], axis=1
                )
            back = back + part
        ret[got, width:] = back.astype(jnp.bfloat16)

    for c in range(CHUNKS):
        low, high = c * per, (c + 1) * per
        if low == half:
            low = low + 1

        @pl.loop(low, high)
        def _(k):
            outward(k).wait_recv()

        work(c)

        @pl.loop(low, high)
        def _(k):
            homeward(k).start()

        if c * per == half:
            out_ref[rows(me), :] = ret[pl.ds(half * BASE, BASE), :]

    @pl.loop(1, n)
    def _(t):
        d = (me + t) % n
        pltpu.make_async_remote_copy(
            src_ref=ret.at[rows(0)],
            dst_ref=out_ref.at[rows(d)],
            send_sem=back_sem.at[0],
            recv_sem=home_sem.at[d],
            device_id=(mine, d),
            device_id_type=MESH,
        ).wait_recv()

    for low, high in ((0, half), (half + 1, n)):

        @pl.loop(low, high)
        def _(k):
            outward(k).wait_send()
            homeward(k).wait_send()


def combine(group, ids_ref, hidden_ref, mod_ref, router_ref, back_ref, mixed_ref):
    width = hidden_ref.shape[1]
    stream = hidden_ref[...].astype(jnp.float32)
    centered = stream - jnp.mean(stream, axis=-1, keepdims=True)
    variance = jnp.mean(centered * centered, axis=-1, keepdims=True)
    normed = centered * lax.rsqrt(variance + 1e-06)
    shift = mod_ref[:, :width]
    scale = mod_ref[:, width : 2 * width]
    current = (normed * (1.0 + scale) + shift).astype(jnp.bfloat16)
    logits = jnp.dot(current, router_ref[...], preferred_element_type=jnp.float32)
    hot, main, rest = keys_of(ids_ref[...])
    picked = [jnp.sum(hot[k] * logits, axis=1, keepdims=True) for k in range(TOP)]
    row = lax.broadcasted_iota(jnp.int32, (stream.shape[0], back_ref.shape[0]), 1)
    table = (row // (BASE * group)) * BASE + row % BASE
    weights = [jax.nn.sigmoid(picked[k] - picked[1 - k]) for k in range(TOP)]
    whole = [onehot(main[k], table) for k in range(TOP)]
    for q, first, size in pieces(width):
        cols = slice(first, first + size)
        routed = jnp.zeros((stream.shape[0], size), jnp.float32)
        for k in range(TOP):
            found = jnp.dot(whole[k], back_ref[:, cols], preferred_element_type=jnp.float32)
            found = found + jnp.dot(
                onehot(rest[k] + q * REST, table), back_ref[:, width : width + size],
                preferred_element_type=jnp.float32,
            )
            routed = routed + weights[k] * found
        gate = mod_ref[:, 2 * width + first : 2 * width + first + size]
        mixed_ref[:, cols] = (hidden_ref[:, cols].astype(jnp.float32) + gate * routed).astype(
            mixed_ref.dtype
        )


def local(
    hidden_now, stale_rows, expert_ids, condition, mod_weight, mod_bias, router, w_gate, w_up, w_down
):
    n = lax.axis_size("seq")
    width = hidden_now.shape[1]
    ff = w_gate.shape[1]
    ff_tile = 512 if ff % 512 == 0 else ff
    d_tile = 256
    message = width + PIECE
    per = n // CHUNKS
    conditioned = jax.nn.silu(condition).astype(jnp.bfloat16)[None, :]
    mod_piece = jnp.dot(conditioned, mod_weight, preferred_element_type=jnp.float32)[0] + mod_bias
    modulation = lax.all_gather(mod_piece, "seq", axis=0, tiled=True)
    vmem = pl.BlockSpec(memory_space=pltpu.VMEM)
    hbm = pl.BlockSpec(memory_space=pl.ANY)
    bf16 = jnp.bfloat16
    back = pl.pallas_call(
        functools.partial(exchange, n, ff_tile, d_tile),
        out_shape=jax.ShapeDtypeStruct((n * BASE, message), bf16),
        in_specs=[vmem, vmem, hbm, hbm, hbm],
        out_specs=vmem,
        scratch_shapes=[
            pltpu.VMEM(w_gate.shape, bf16),
            pltpu.VMEM(w_up.shape, bf16),
            pltpu.VMEM(w_down.shape, bf16),
            pltpu.VMEM((EXPERTS * BASE, message), bf16),
            pltpu.VMEM((n * BASE, message), bf16),
            pltpu.VMEM((n * BASE, message), bf16),
            pltpu.VMEM((per * CAP, width), bf16),
            pltpu.VMEM((per * CAP, ff), bf16),
            pltpu.SemaphoreType.DMA((3,)),
            pltpu.SemaphoreType.DMA((n,)),
            pltpu.SemaphoreType.DMA((n,)),
            pltpu.SemaphoreType.DMA((n,)),
            pltpu.SemaphoreType.DMA((n,)),
        ],
        compiler_params=pltpu.CompilerParams(
            collective_id=0, has_side_effects=True, vmem_limit_bytes=58 * 1024 * 1024
        ),
        cost_estimate=pl.CostEstimate(
            flops=6 * n * CAP * width * ff, bytes_accessed=6 * width * ff, transcendentals=0
        ),
        name="exchange",
    )(expert_ids, stale_rows, w_gate, w_up, w_down)
    return pl.pallas_call(
        functools.partial(combine, n // EXPERTS),
        out_shape=jax.ShapeDtypeStruct(hidden_now.shape, hidden_now.dtype),
        in_specs=[vmem] * 5,
        out_specs=vmem,
        compiler_params=pltpu.CompilerParams(vmem_limit_bytes=48 * 1024 * 1024),
        name="combine",
    )(expert_ids, hidden_now, modulation[None, :], router, back)


def solution(mesh):
    in_specs = (
        P(("groups", "seq"), None),
        P(("groups", "seq"), None),
        P(("groups", "seq"), None),
        P("groups"),
        P(None, "seq"),
        P("seq"),
        P(),
        P(None, "seq"),
        P(None, "seq"),
        P("seq", None),
    )
    out_specs = P(("groups", "seq"), None)
    return jax.shard_map(local, mesh=mesh, in_specs=in_specs, out_specs=out_specs, check_vma=False)
```

```python
import functools

import jax
import jax.numpy as jnp
from jax import lax
from jax.experimental import pallas as pl
from jax.experimental.pallas import tpu as pltpu
from jax.sharding import PartitionSpec as P

EXPERTS = 16
TOP = 2
CAP = 20
BASE = 16
REST = CAP - BASE
PARTS = BASE // REST
PIECE = 512
CHUNKS = 4
MESH = pl.DeviceIdType.MESH


def pieces(width):
    return [(q, q * PIECE, min(PIECE, width - q * PIECE)) for q in range(PARTS)]


def keys_of(ids):
    rows = ids.shape[0]
    experts = lax.broadcasted_iota(jnp.int32, (rows, EXPERTS), 1)
    hot = [(ids[:, k : k + 1] == experts).astype(jnp.float32) for k in range(TOP)]
    below = (
        lax.broadcasted_iota(jnp.int32, (rows, rows), 1)
        < lax.broadcasted_iota(jnp.int32, (rows, rows), 0)
    ).astype(jnp.bfloat16)
    before = jnp.dot(
        below, (hot[0] + hot[1]).astype(jnp.bfloat16), preferred_element_type=jnp.float32
    )
    main, rest = [], []
    for k in range(TOP):
        slot = jnp.sum(hot[k] * before, axis=1, keepdims=True).astype(jnp.int32)
        first = ids[:, k : k + 1] * BASE + slot
        main.append(jnp.where(slot < BASE, first, -1))
        rest.append(jnp.where(slot >= BASE, first - BASE, -(EXPERTS + 1) * BASE))
    return hot, main, rest


def onehot(key, table):
    return (key == table).astype(jnp.float32).astype(jnp.bfloat16)


def exchange(
    n, ff_tile, d_tile, ids_ref, stale_ref, hidden_ref, cond_ref, bias_ref, router_ref,
    mw_hbm, wg_hbm, wu_hbm, wd_hbm, mixed_ref,
    mw, wg, wu, wd, send, recv, ret, out_ref, xbuf, act, mod_own, mod_all,
    w_sem, out_sem, in_sem, back_sem, home_sem, mod_out_sem, mod_in_sem,
):
    width = stale_ref.shape[1]
    ff = wg.shape[1]
    group = n // EXPERTS
    half = n // 2
    per = n // CHUNKS
    me = lax.axis_index("seq")
    mine = lax.axis_index("groups")
    side, place = me // half, me % half

    loads = [
        pltpu.make_async_copy(src, dst, w_sem.at[i])
        for i, (src, dst) in enumerate(
            ((wg_hbm, wg), (wu_hbm, wu), (wd_hbm, wd), (mw_hbm, mw))
        )
    ]
    for i in (3, 0, 1, 2):
        loads[i].start()

    def target(k):
        far = (1 - side) * half + (place + k) % half
        near = side * half + (place + k) % half
        return jnp.where(k < half, far, near)

    def source(k):
        far = (1 - side) * half + (place + 2 * half - k) % half
        near = side * half + (place + 2 * half - k) % half
        return jnp.where(k < half, far, near)

    def rows(k):
        return pl.ds(pl.multiple_of(k * BASE, BASE), BASE)

    def outward(k):
        to = target(k)
        return pltpu.make_async_remote_copy(
            src_ref=send.at[rows(to // group)],
            dst_ref=recv.at[rows(k)],
            send_sem=out_sem.at[k],
            recv_sem=in_sem.at[k],
            device_id=(mine, to),
            device_id_type=MESH,
        )

    def homeward(k):
        return pltpu.make_async_remote_copy(
            src_ref=ret.at[rows(k)],
            dst_ref=out_ref.at[rows(me)],
            send_sem=back_sem.at[k],
            recv_sem=home_sem.at[me],
            device_id=(mine, source(k)),
            device_id_type=MESH,
        )

    def strip(d):
        return pl.ds(pl.multiple_of(d * 8, 8), 8)

    def modward(k):
        return pltpu.make_async_remote_copy(
            src_ref=mod_own,
            dst_ref=mod_all.at[strip(me)],
            send_sem=mod_out_sem.at[k],
            recv_sem=mod_in_sem.at[me],
            device_id=(mine, target(k)),
            device_id_type=MESH,
        )

    barrier = pltpu.get_barrier_semaphore()

    @pl.loop(1, n)
    def _(t):
        pl.semaphore_signal(
            barrier, inc=1, device_id=(mine, (me + t) % n), device_id_type=MESH
        )

    hot, main, rest = keys_of(ids_ref[...])
    stale = stale_ref[...]
    table = lax.broadcasted_iota(jnp.int32, (stale.shape[0], EXPERTS * BASE), 1)
    over_rows = (((0,), (0,)), ((), ()))
    pick = onehot(main[0], table) + onehot(main[1], table)
    send[:, :width] = lax.dot_general(
        pick, stale, over_rows, preferred_element_type=jnp.float32
    ).astype(jnp.bfloat16)
    tail = jnp.zeros((EXPERTS * BASE, PIECE), jnp.float32)
    for q, first, size in pieces(width):
        pick = onehot(rest[0] + q * REST, table) + onehot(rest[1] + q * REST, table)
        part = lax.dot_general(
            pick, stale[:, first : first + size], over_rows, preferred_element_type=jnp.float32
        )
        if size < PIECE:
            part = jnp.concatenate(
                [part, jnp.zeros((part.shape[0], PIECE - size), jnp.float32)], axis=1
            )
        tail = tail + part
    send[:, width:] = tail.astype(jnp.bfloat16)

    pl.semaphore_wait(barrier, n - 1)

    @pl.loop(0, half)
    def _(k):
        outward(k).start()

    @pl.loop(half + 1, n)
    def _(k):
        outward(k).start()

    recv[pl.ds(half * BASE, BASE), :] = send[rows(me // group), :]

    loads[3].wait()
    conditioned = jax.nn.silu(cond_ref[...]).astype(jnp.bfloat16)
    piece = bias_ref.shape[1]
    own = jnp.dot(conditioned, mw[...], preferred_element_type=jnp.float32) + bias_ref[...]
    mod_own[...] = jnp.zeros(mod_own.shape, jnp.float32)
    mod_own[0:1, :piece] = own
    mod_all[strip(me), :] = mod_own[...]

    @pl.loop(0, half)
    def _(k):
        modward(k).start()

    @pl.loop(half + 1, n)
    def _(k):
        modward(k).start()

    def work(c):
        base = c * per * BASE
        count = per * BASE
        extra = per * REST
        got = pl.ds(base, count)
        xbuf[:count] = recv[got, :width]
        across = lax.broadcasted_iota(jnp.int32, (extra, count), 1)
        down = lax.broadcasted_iota(jnp.int32, (extra, count), 0)
        spread = (down // REST) * BASE + down % REST
        tails = recv[got, width:]
        for q, first, size in pieces(width):
            xbuf[count:, first : first + size] = jnp.dot(
                onehot(spread + q * REST, across), tails[:, :size],
                preferred_element_type=jnp.float32,
            ).astype(jnp.bfloat16)
        if c == 0:
            loads[0].wait()
            loads[1].wait()

        @pl.loop(0, ff // ff_tile)
        def _(j):
            cols = pl.ds(pl.multiple_of(j * ff_tile, ff_tile), ff_tile)
            gate = jnp.dot(xbuf[...], wg[:, cols], preferred_element_type=jnp.float32)
            up = jnp.dot(xbuf[...], wu[:, cols], preferred_element_type=jnp.float32)
            act[:, cols] = (jax.nn.silu(gate) * up).astype(jnp.bfloat16)

        if c == 0:
            loads[2].wait()

        @pl.loop(0, width // d_tile)
        def _(j):
            cols = pl.ds(pl.multiple_of(j * d_tile, d_tile), d_tile)
            xbuf[:, cols] = jnp.dot(
                act[...], wd[:, cols], preferred_element_type=jnp.float32
            ).astype(jnp.bfloat16)

        ret[got, :width] = xbuf[:count]
        across = lax.broadcasted_iota(jnp.int32, (count, extra), 1)
        down = lax.broadcasted_iota(jnp.int32, (count, extra), 0)
        spread = (across // REST) * BASE + across % REST
        back = jnp.zeros((count, PIECE), jnp.float32)
        for q, first, size in pieces(width):
            part = jnp.dot(
                onehot(spread + q * REST, down), xbuf[count:, first : first + size],
                preferred_element_type=jnp.float32,
            )
            if size < PIECE:
                part = jnp.concatenate(
                    [part, jnp.zeros((count, PIECE - size), jnp.float32)], axis=1
                )
            back = back + part
        ret[got, width:] = back.astype(jnp.bfloat16)

    for c in range(CHUNKS):
        low, high = c * per, (c + 1) * per
        if low == half:
            low = low + 1

        @pl.loop(low, high)
        def _(k):
            outward(k).wait_recv()

        work(c)

        @pl.loop(low, high)
        def _(k):
            homeward(k).start()

        if c * per == half:
            out_ref[rows(me), :] = ret[pl.ds(half * BASE, BASE), :]

    @pl.loop(1, n)
    def _(t):
        d = (me + t) % n
        pltpu.make_async_remote_copy(
            src_ref=mod_own,
            dst_ref=mod_all.at[strip(d)],
            send_sem=mod_out_sem.at[0],
            recv_sem=mod_in_sem.at[d],
            device_id=(mine, d),
            device_id_type=MESH,
        ).wait_recv()

    stream = hidden_ref[...].astype(jnp.float32)
    centered = stream - jnp.mean(stream, axis=-1, keepdims=True)
    variance = jnp.mean(centered * centered, axis=-1, keepdims=True)
    normed = centered * lax.rsqrt(variance + 1e-06)
    modulation = jnp.concatenate([mod_all[d * 8 : d * 8 + 1, :piece] for d in range(n)], axis=1)
    shift = modulation[:, :width]
    scale = modulation[:, width : 2 * width]
    current = (normed * (1.0 + scale) + shift).astype(jnp.bfloat16)
    logits = jnp.dot(current, router_ref[...], preferred_element_type=jnp.float32)
    picked = [jnp.sum(hot[k] * logits, axis=1, keepdims=True) for k in range(TOP)]
    weights = [jax.nn.sigmoid(picked[k] - picked[1 - k]) for k in range(TOP)]
    row = lax.broadcasted_iota(jnp.int32, (stream.shape[0], n * BASE), 1)
    table = (row // (BASE * group)) * BASE + row % BASE
    whole = [onehot(main[k], table) for k in range(TOP)]

    @pl.loop(1, n)
    def _(t):
        d = (me + t) % n
        pltpu.make_async_remote_copy(
            src_ref=ret.at[rows(0)],
            dst_ref=out_ref.at[rows(d)],
            send_sem=back_sem.at[0],
            recv_sem=home_sem.at[d],
            device_id=(mine, d),
            device_id_type=MESH,
        ).wait_recv()

    for q, first, size in pieces(width):
        cols = slice(first, first + size)
        routed = jnp.zeros((stream.shape[0], size), jnp.float32)
        for k in range(TOP):
            found = jnp.dot(whole[k], out_ref[:, cols], preferred_element_type=jnp.float32)
            found = found + jnp.dot(
                onehot(rest[k] + q * REST, table), out_ref[:, width : width + size],
                preferred_element_type=jnp.float32,
            )
            routed = routed + weights[k] * found
        gate = modulation[:, 2 * width + first : 2 * width + first + size]
        mixed_ref[:, cols] = (hidden_ref[:, cols].astype(jnp.float32) + gate * routed).astype(
            mixed_ref.dtype
        )

    for low, high in ((0, half), (half + 1, n)):

        @pl.loop(low, high)
        def _(k):
            outward(k).wait_send()
            modward(k).wait_send()
            homeward(k).wait_send()


def local(
    hidden_now, stale_rows, expert_ids, condition, mod_weight, mod_bias, router, w_gate, w_up, w_down
):
    n = lax.axis_size("seq")
    width = hidden_now.shape[1]
    ff = w_gate.shape[1]
    ff_tile = 512 if ff % 512 == 0 else ff
    d_tile = 256
    message = width + PIECE
    per = n // CHUNKS
    piece = mod_bias.shape[0]
    lanes = -(-piece // 128) * 128
    vmem = pl.BlockSpec(memory_space=pltpu.VMEM)
    hbm = pl.BlockSpec(memory_space=pl.ANY)
    bf16 = jnp.bfloat16
    return pl.pallas_call(
        functools.partial(exchange, n, ff_tile, d_tile),
        out_shape=jax.ShapeDtypeStruct(hidden_now.shape, hidden_now.dtype),
        in_specs=[vmem] * 6 + [hbm] * 4,
        out_specs=vmem,
        scratch_shapes=[
            pltpu.VMEM(mod_weight.shape, bf16),
            pltpu.VMEM(w_gate.shape, bf16),
            pltpu.VMEM(w_up.shape, bf16),
            pltpu.VMEM(w_down.shape, bf16),
            pltpu.VMEM((EXPERTS * BASE, message), bf16),
            pltpu.VMEM((n * BASE, message), bf16),
            pltpu.VMEM((n * BASE, message), bf16),
            pltpu.VMEM((n * BASE, message), bf16),
            pltpu.VMEM((per * CAP, width), bf16),
            pltpu.VMEM((per * CAP, ff), bf16),
            pltpu.VMEM((8, lanes), jnp.float32),
            pltpu.VMEM((n * 8, lanes), jnp.float32),
            pltpu.SemaphoreType.DMA((4,)),
            pltpu.SemaphoreType.DMA((n,)),
            pltpu.SemaphoreType.DMA((n,)),
            pltpu.SemaphoreType.DMA((n,)),
            pltpu.SemaphoreType.DMA((n,)),
            pltpu.SemaphoreType.DMA((n,)),
            pltpu.SemaphoreType.DMA((n,)),
        ],
        compiler_params=pltpu.CompilerParams(
            collective_id=0, has_side_effects=True, vmem_limit_bytes=58 * 1024 * 1024
        ),
        cost_estimate=pl.CostEstimate(
            flops=6 * n * CAP * width * ff, bytes_accessed=6 * width * ff, transcendentals=0
        ),
        name="exchange",
    )(
        expert_ids, stale_rows, hidden_now, condition[None, :], mod_bias[None, :], router,
        mod_weight, w_gate, w_up, w_down,
    )


def solution(mesh):
    in_specs = (
        P(("groups", "seq"), None),
        P(("groups", "seq"), None),
        P(("groups", "seq"), None),
        P("groups"),
        P(None, "seq"),
        P("seq"),
        P(),
        P(None, "seq"),
        P(None, "seq"),
        P("seq", None),
    )
    out_specs = P(("groups", "seq"), None)
    return jax.shard_map(local, mesh=mesh, in_specs=in_specs, out_specs=out_specs, check_vma=False)
```

```python
import functools

import jax
import jax.numpy as jnp
from jax import lax
from jax.experimental import pallas as pl
from jax.experimental.pallas import tpu as pltpu
from jax.sharding import PartitionSpec as P

EXPERTS = 16
TOP = 2
CAP = 20
BASE = 16
REST = CAP - BASE
PARTS = BASE // REST
PIECE = 512
CHUNKS = 2
MESH = pl.DeviceIdType.MESH


def pieces(width):
    return [(q, q * PIECE, min(PIECE, width - q * PIECE)) for q in range(PARTS)]


def keys_of(ids):
    rows = ids.shape[1]
    experts = lax.broadcasted_iota(jnp.int32, (EXPERTS, rows), 0)
    hot = [(ids[k : k + 1, :] == experts).astype(jnp.float32) for k in range(TOP)]
    earlier = (
        lax.broadcasted_iota(jnp.int32, (rows, rows), 0)
        < lax.broadcasted_iota(jnp.int32, (rows, rows), 1)
    ).astype(jnp.float32).astype(jnp.bfloat16)
    before = jnp.dot(
        (hot[0] + hot[1]).astype(jnp.bfloat16), earlier, preferred_element_type=jnp.float32
    )
    main, rest = [], []
    for k in range(TOP):
        slot = jnp.sum(hot[k] * before, axis=0, keepdims=True).astype(jnp.int32)
        first = ids[k : k + 1, :] * BASE + slot
        main.append(jnp.where(slot < BASE, first, -1))
        rest.append(jnp.where(slot >= BASE, first - BASE, -(EXPERTS + 1) * BASE))
    return hot, main, rest


def onehot(key, table):
    return (key == table).astype(jnp.float32).astype(jnp.bfloat16)


def exchange(
    n, ff_tile, d_tile, ids_ref, stale_ref, hidden_ref, cond_ref, bias_ref, router_ref,
    mw_hbm, wg_hbm, wu_hbm, wd_hbm, mixed_ref,
    mw, wg, wu, wd, send, recv, ret, out_ref, xbuf, act, mod_own, mod_all,
    w_sem, out_sem, in_sem, back_sem, home_sem, mod_out_sem, mod_in_sem,
):
    width = stale_ref.shape[1]
    ff = wg.shape[1]
    group = n // EXPERTS
    half = n // 2
    per = n // CHUNKS
    me = lax.axis_index("seq")
    mine = lax.axis_index("groups")
    side, place = me // half, me % half

    loads = [
        pltpu.make_async_copy(src, dst, w_sem.at[i])
        for i, (src, dst) in enumerate(
            ((wg_hbm, wg), (wu_hbm, wu), (wd_hbm, wd), (mw_hbm, mw))
        )
    ]
    for i in (3, 0, 1, 2):
        loads[i].start()

    def target(k):
        far = (1 - side) * half + (place + k) % half
        near = side * half + (place + k) % half
        return jnp.where(k < half, far, near)

    def source(k):
        far = (1 - side) * half + (place + 2 * half - k) % half
        near = side * half + (place + 2 * half - k) % half
        return jnp.where(k < half, far, near)

    def rows(k):
        return pl.ds(pl.multiple_of(k * BASE, BASE), BASE)

    def outward(k):
        to = target(k)
        return pltpu.make_async_remote_copy(
            src_ref=send.at[rows(to // group)],
            dst_ref=recv.at[rows(k)],
            send_sem=out_sem.at[k],
            recv_sem=in_sem.at[k],
            device_id=(mine, to),
            device_id_type=MESH,
        )

    def homeward(k):
        return pltpu.make_async_remote_copy(
            src_ref=ret.at[rows(k)],
            dst_ref=out_ref.at[rows(me)],
            send_sem=back_sem.at[k],
            recv_sem=home_sem.at[me],
            device_id=(mine, source(k)),
            device_id_type=MESH,
        )

    def strip(d):
        return pl.ds(pl.multiple_of(d * 8, 8), 8)

    def modward(k):
        return pltpu.make_async_remote_copy(
            src_ref=mod_own,
            dst_ref=mod_all.at[strip(me)],
            send_sem=mod_out_sem.at[k],
            recv_sem=mod_in_sem.at[me],
            device_id=(mine, target(k)),
            device_id_type=MESH,
        )

    barrier = pltpu.get_barrier_semaphore()

    @pl.loop(1, n)
    def _(t):
        pl.semaphore_signal(
            barrier, inc=1, device_id=(mine, (me + t) % n), device_id_type=MESH
        )

    hot, main, rest = keys_of(ids_ref[...])
    stale = stale_ref[...]
    table = lax.broadcasted_iota(jnp.int32, (EXPERTS * BASE, stale.shape[0]), 0)
    over_rows = (((0,), (0,)), ((), ()))
    pick = onehot(main[0], table) + onehot(main[1], table)
    send[:, :width] = jnp.dot(
        pick, stale, preferred_element_type=jnp.float32
    ).astype(jnp.bfloat16)
    tail = jnp.zeros((EXPERTS * BASE, PIECE), jnp.float32)
    for q, first, size in pieces(width):
        pick = onehot(rest[0] + q * REST, table) + onehot(rest[1] + q * REST, table)
        part = jnp.dot(
            pick, stale[:, first : first + size], preferred_element_type=jnp.float32
        )
        if size < PIECE:
            part = jnp.concatenate(
                [part, jnp.zeros((part.shape[0], PIECE - size), jnp.float32)], axis=1
            )
        tail = tail + part
    send[:, width:] = tail.astype(jnp.bfloat16)

    pl.semaphore_wait(barrier, n - 1)

    @pl.loop(0, half)
    def _(k):
        outward(k).start()

    @pl.loop(half + 1, n)
    def _(k):
        outward(k).start()

    recv[pl.ds(half * BASE, BASE), :] = send[rows(me // group), :]

    loads[3].wait()
    conditioned = jax.nn.silu(cond_ref[...].reshape(1, -1)).astype(jnp.bfloat16)
    piece = bias_ref.shape[0]
    over_features = (((1,), (1,)), ((), ()))
    own = lax.dot_general(
        conditioned, mw[...], over_features, preferred_element_type=jnp.float32
    ) + bias_ref[...].reshape(1, -1)
    mod_own[...] = jnp.zeros(mod_own.shape, jnp.float32)
    mod_own[0:1, :piece] = own
    mod_all[strip(me), :] = mod_own[...]

    @pl.loop(0, half)
    def _(k):
        modward(k).start()

    @pl.loop(half + 1, n)
    def _(k):
        modward(k).start()

    def work(c):
        base = c * per * BASE
        count = per * BASE
        extra = per * REST
        got = pl.ds(base, count)
        xbuf[:count] = recv[got, :width]
        across = lax.broadcasted_iota(jnp.int32, (extra, count), 1)
        down = lax.broadcasted_iota(jnp.int32, (extra, count), 0)
        spread = (down // REST) * BASE + down % REST
        tails = recv[got, width:]
        for q, first, size in pieces(width):
            xbuf[count:, first : first + size] = jnp.dot(
                onehot(spread + q * REST, across), tails[:, :size],
                preferred_element_type=jnp.float32,
            ).astype(jnp.bfloat16)
        if c == 0:
            loads[0].wait()
            loads[1].wait()

        @pl.loop(0, ff // ff_tile)
        def _(j):
            cols = pl.ds(pl.multiple_of(j * ff_tile, ff_tile), ff_tile)
            gate = jnp.dot(xbuf[...], wg[:, cols], preferred_element_type=jnp.float32)
            up = jnp.dot(xbuf[...], wu[:, cols], preferred_element_type=jnp.float32)
            act[:, cols] = (jax.nn.silu(gate) * up).astype(jnp.bfloat16)

        if c == 0:
            loads[2].wait()

        @pl.loop(0, width // d_tile)
        def _(j):
            cols = pl.ds(pl.multiple_of(j * d_tile, d_tile), d_tile)
            xbuf[:, cols] = jnp.dot(
                act[...], wd[:, cols], preferred_element_type=jnp.float32
            ).astype(jnp.bfloat16)

        ret[got, :width] = xbuf[:count]
        across = lax.broadcasted_iota(jnp.int32, (count, extra), 1)
        down = lax.broadcasted_iota(jnp.int32, (count, extra), 0)
        spread = (across // REST) * BASE + across % REST
        back = jnp.zeros((count, PIECE), jnp.float32)
        for q, first, size in pieces(width):
            part = jnp.dot(
                onehot(spread + q * REST, down), xbuf[count:, first : first + size],
                preferred_element_type=jnp.float32,
            )
            if size < PIECE:
                part = jnp.concatenate(
                    [part, jnp.zeros((count, PIECE - size), jnp.float32)], axis=1
                )
            back = back + part
        ret[got, width:] = back.astype(jnp.bfloat16)

    for c in range(CHUNKS):
        low, high = c * per, (c + 1) * per
        if low == half:
            low = low + 1

        @pl.loop(low, high)
        def _(k):
            outward(k).wait_recv()

        work(c)

        @pl.loop(low, high)
        def _(k):
            homeward(k).start()

        if c * per == half:
            out_ref[rows(me), :] = ret[pl.ds(half * BASE, BASE), :]

    @pl.loop(1, n)
    def _(t):
        d = (me + t) % n
        pltpu.make_async_remote_copy(
            src_ref=mod_own,
            dst_ref=mod_all.at[strip(d)],
            send_sem=mod_out_sem.at[0],
            recv_sem=mod_in_sem.at[d],
            device_id=(mine, d),
            device_id_type=MESH,
        ).wait_recv()

    stream = hidden_ref[...].astype(jnp.float32)
    centered = stream - jnp.mean(stream, axis=-1, keepdims=True)
    variance = jnp.mean(centered * centered, axis=-1, keepdims=True)
    normed = centered * lax.rsqrt(variance + 1e-06)
    modulation = jnp.concatenate([mod_all[d * 8 : d * 8 + 1, :piece] for d in range(n)], axis=1)
    shift = modulation[:, :width]
    scale = modulation[:, width : 2 * width]
    current = (normed * (1.0 + scale) + shift).astype(jnp.bfloat16)
    logits = lax.dot_general(
        router_ref[...], current, over_features, preferred_element_type=jnp.float32
    )
    picked = [jnp.sum(hot[k] * logits, axis=0, keepdims=True) for k in range(TOP)]
    weights = [
        jnp.broadcast_to(jax.nn.sigmoid(picked[k] - picked[1 - k]), (128, stream.shape[0])).T[:, :1]
        for k in range(TOP)
    ]
    row = lax.broadcasted_iota(jnp.int32, (n * BASE, stream.shape[0]), 0)
    table = (row // (BASE * group)) * BASE + row % BASE
    whole = [onehot(main[k], table) for k in range(TOP)]

    @pl.loop(1, n)
    def _(t):
        d = (me + t) % n
        pltpu.make_async_remote_copy(
            src_ref=ret.at[rows(0)],
            dst_ref=out_ref.at[rows(d)],
            send_sem=back_sem.at[0],
            recv_sem=home_sem.at[d],
            device_id=(mine, d),
            device_id_type=MESH,
        ).wait_recv()

    for q, first, size in pieces(width):
        cols = slice(first, first + size)
        routed = jnp.zeros((stream.shape[0], size), jnp.float32)
        for k in range(TOP):
            found = lax.dot_general(
                whole[k], out_ref[:, cols], over_rows, preferred_element_type=jnp.float32
            )
            found = found + lax.dot_general(
                onehot(rest[k] + q * REST, table), out_ref[:, width : width + size],
                over_rows, preferred_element_type=jnp.float32,
            )
            routed = routed + weights[k] * found
        gate = modulation[:, 2 * width + first : 2 * width + first + size]
        mixed_ref[:, cols] = (hidden_ref[:, cols].astype(jnp.float32) + gate * routed).astype(
            mixed_ref.dtype
        )

    for low, high in ((0, half), (half + 1, n)):

        @pl.loop(low, high)
        def _(k):
            outward(k).wait_send()
            modward(k).wait_send()
            homeward(k).wait_send()


def local(
    hidden_now, stale_rows, expert_ids, condition, mod_weight, mod_bias, router, w_gate, w_up, w_down
):
    n = lax.axis_size("seq")
    width = hidden_now.shape[1]
    ff = w_gate.shape[1]
    ff_tile = 512 if ff % 512 == 0 else ff
    d_tile = 256
    message = width + PIECE
    per = n // CHUNKS
    piece = mod_bias.shape[0]
    lanes = -(-piece // 128) * 128
    vmem = pl.BlockSpec(memory_space=pltpu.VMEM)
    hbm = pl.BlockSpec(memory_space=pl.ANY)
    bf16 = jnp.bfloat16
    return pl.pallas_call(
        functools.partial(exchange, n, ff_tile, d_tile),
        out_shape=jax.ShapeDtypeStruct(hidden_now.shape, hidden_now.dtype),
        in_specs=[vmem] * 6 + [hbm] * 4,
        out_specs=vmem,
        scratch_shapes=[
            pltpu.VMEM(mod_weight.shape[::-1], bf16),
            pltpu.VMEM(w_gate.shape, bf16),
            pltpu.VMEM(w_up.shape, bf16),
            pltpu.VMEM(w_down.shape, bf16),
            pltpu.VMEM((EXPERTS * BASE, message), bf16),
            pltpu.VMEM((n * BASE, message), bf16),
            pltpu.VMEM((n * BASE, message), bf16),
            pltpu.VMEM((n * BASE, message), bf16),
            pltpu.VMEM((per * CAP, width), bf16),
            pltpu.VMEM((per * CAP, ff), bf16),
            pltpu.VMEM((8, lanes), jnp.float32),
            pltpu.VMEM((n * 8, lanes), jnp.float32),
            pltpu.SemaphoreType.DMA((4,)),
            pltpu.SemaphoreType.DMA((n,)),
            pltpu.SemaphoreType.DMA((n,)),
            pltpu.SemaphoreType.DMA((n,)),
            pltpu.SemaphoreType.DMA((n,)),
            pltpu.SemaphoreType.DMA((n,)),
            pltpu.SemaphoreType.DMA((n,)),
        ],
        compiler_params=pltpu.CompilerParams(
            collective_id=0, has_side_effects=True, vmem_limit_bytes=58 * 1024 * 1024
        ),
        cost_estimate=pl.CostEstimate(
            flops=6 * n * CAP * width * ff, bytes_accessed=6 * width * ff, transcendentals=0
        ),
        name="exchange",
    )(
        expert_ids.T, stale_rows, hidden_now, condition, mod_bias, router.T,
        mod_weight.T, w_gate, w_up, w_down,
    )


def solution(mesh):
    in_specs = (
        P(("groups", "seq"), None),
        P(("groups", "seq"), None),
        P(("groups", "seq"), None),
        P("groups"),
        P(None, "seq"),
        P("seq"),
        P(),
        P(None, "seq"),
        P(None, "seq"),
        P("seq", None),
    )
    out_specs = P(("groups", "seq"), None)
    return jax.shard_map(local, mesh=mesh, in_specs=in_specs, out_specs=out_specs, check_vma=False)
```

```python
import functools

import jax
import jax.numpy as jnp
from jax import lax
from jax.experimental import pallas as pl
from jax.experimental.pallas import tpu as pltpu
from jax.sharding import PartitionSpec as P

EXPERTS = 16
TOP = 2
CAP = 20
BASE = 16
REST = CAP - BASE
PARTS = BASE // REST
PIECE = 512
CHUNKS = ((0, 4), (8, 8), (4, 4))
MESH = pl.DeviceIdType.MESH


def pieces(width):
    return [(q, q * PIECE, min(PIECE, width - q * PIECE)) for q in range(PARTS)]


def keys_of(ids):
    rows = ids.shape[1]
    experts = lax.broadcasted_iota(jnp.int32, (EXPERTS, rows), 0)
    hot = [(ids[k : k + 1, :] == experts).astype(jnp.float32) for k in range(TOP)]
    earlier = (
        lax.broadcasted_iota(jnp.int32, (rows, rows), 0)
        < lax.broadcasted_iota(jnp.int32, (rows, rows), 1)
    ).astype(jnp.float32).astype(jnp.bfloat16)
    before = jnp.dot(
        (hot[0] + hot[1]).astype(jnp.bfloat16), earlier, preferred_element_type=jnp.float32
    )
    main, rest = [], []
    for k in range(TOP):
        slot = jnp.sum(hot[k] * before, axis=0, keepdims=True).astype(jnp.int32)
        first = ids[k : k + 1, :] * BASE + slot
        main.append(jnp.where(slot < BASE, first, -1))
        rest.append(jnp.where(slot >= BASE, first - BASE, -(EXPERTS + 1) * BASE))
    return hot, main, rest


def onehot(key, table):
    return (key == table).astype(jnp.float32).astype(jnp.bfloat16)


def exchange(
    n, ff_tile, d_tile, ids_ref, stale_ref, hidden_ref, cond_ref, bias_ref, router_ref,
    mw_hbm, wg_hbm, wu_hbm, wd_hbm, mixed_ref,
    mw, wg, wu, wd, send, recv, ret, out_ref, xbuf, act, mod_own, mod_all,
    w_sem, out_sem, in_sem, back_sem, home_sem, mod_out_sem, mod_in_sem,
):
    width = stale_ref.shape[1]
    ff = wg.shape[1]
    group = n // EXPERTS
    half = n // 2
    me = lax.axis_index("seq")
    mine = lax.axis_index("groups")
    side, place = me // half, me % half

    loads = [
        pltpu.make_async_copy(src, dst, w_sem.at[i])
        for i, (src, dst) in enumerate(
            ((wg_hbm, wg), (wu_hbm, wu), (wd_hbm, wd), (mw_hbm, mw))
        )
    ]
    for i in (3, 0, 1, 2):
        loads[i].start()

    def target(k):
        far = (1 - side) * half + (place + k) % half
        near = side * half + (place + k) % half
        return jnp.where(k < half, far, near)

    def source(k):
        far = (1 - side) * half + (place + 2 * half - k) % half
        near = side * half + (place + 2 * half - k) % half
        return jnp.where(k < half, far, near)

    def rows(k):
        return pl.ds(pl.multiple_of(k * BASE, BASE), BASE)

    def outward(k):
        to = target(k)
        return pltpu.make_async_remote_copy(
            src_ref=send.at[rows(to // group)],
            dst_ref=recv.at[rows(k)],
            send_sem=out_sem.at[k],
            recv_sem=in_sem.at[k],
            device_id=(mine, to),
            device_id_type=MESH,
        )

    def homeward(k):
        return pltpu.make_async_remote_copy(
            src_ref=ret.at[rows(k)],
            dst_ref=out_ref.at[rows(me)],
            send_sem=back_sem.at[k],
            recv_sem=home_sem.at[me],
            device_id=(mine, source(k)),
            device_id_type=MESH,
        )

    def strip(d):
        return pl.ds(pl.multiple_of(d * 8, 8), 8)

    def modward(k):
        return pltpu.make_async_remote_copy(
            src_ref=mod_own,
            dst_ref=mod_all.at[strip(me)],
            send_sem=mod_out_sem.at[k],
            recv_sem=mod_in_sem.at[me],
            device_id=(mine, target(k)),
            device_id_type=MESH,
        )

    barrier = pltpu.get_barrier_semaphore()

    @pl.loop(1, n)
    def _(t):
        pl.semaphore_signal(
            barrier, inc=1, device_id=(mine, (me + t) % n), device_id_type=MESH
        )

    hot, main, rest = keys_of(ids_ref[...])
    stale = stale_ref[...]
    table = lax.broadcasted_iota(jnp.int32, (EXPERTS * BASE, stale.shape[0]), 0)
    over_rows = (((0,), (0,)), ((), ()))
    pick = onehot(main[0], table) + onehot(main[1], table)
    send[:, :width] = jnp.dot(
        pick, stale, preferred_element_type=jnp.float32
    ).astype(jnp.bfloat16)
    tail = jnp.zeros((EXPERTS * BASE, PIECE), jnp.float32)
    for q, first, size in pieces(width):
        pick = onehot(rest[0] + q * REST, table) + onehot(rest[1] + q * REST, table)
        part = jnp.dot(
            pick, stale[:, first : first + size], preferred_element_type=jnp.float32
        )
        if size < PIECE:
            part = jnp.concatenate(
                [part, jnp.zeros((part.shape[0], PIECE - size), jnp.float32)], axis=1
            )
        tail = tail + part
    send[:, width:] = tail.astype(jnp.bfloat16)

    pl.semaphore_wait(barrier, n - 1)

    @pl.loop(0, half // 2)
    def _(k):
        outward(k).start()

    @pl.loop(half + 1, n)
    def _(k):
        outward(k).start()

    recv[pl.ds(half * BASE, BASE), :] = send[rows(me // group), :]

    loads[3].wait()
    conditioned = jax.nn.silu(cond_ref[...].reshape(1, -1)).astype(jnp.bfloat16)
    piece = bias_ref.shape[0]
    over_features = (((1,), (1,)), ((), ()))
    own = lax.dot_general(
        conditioned, mw[...], over_features, preferred_element_type=jnp.float32
    ) + bias_ref[...].reshape(1, -1)
    mod_own[...] = jnp.zeros(mod_own.shape, jnp.float32)
    mod_own[0:1, :piece] = own
    mod_all[strip(me), :] = mod_own[...]

    @pl.loop(0, half)
    def _(k):
        modward(k).start()

    @pl.loop(half + 1, n)
    def _(k):
        modward(k).start()

    @pl.loop(0, half // 2)
    def _(k):
        outward(k).wait_send()

    @pl.loop(half // 2, half)
    def _(k):
        outward(k).start()

    def work(low, per, is_first):
        base = low * BASE
        count = per * BASE
        extra = per * REST
        got = pl.ds(base, count)
        used = pl.ds(0, count + extra)
        xbuf[:count] = recv[got, :width]
        across = lax.broadcasted_iota(jnp.int32, (extra, count), 1)
        down = lax.broadcasted_iota(jnp.int32, (extra, count), 0)
        spread = (down // REST) * BASE + down % REST
        tails = recv[got, width:]
        for q, first, size in pieces(width):
            xbuf[count : count + extra, first : first + size] = jnp.dot(
                onehot(spread + q * REST, across), tails[:, :size],
                preferred_element_type=jnp.float32,
            ).astype(jnp.bfloat16)
        if is_first:
            loads[0].wait()
            loads[1].wait()

        @pl.loop(0, ff // ff_tile)
        def _(j):
            cols = pl.ds(pl.multiple_of(j * ff_tile, ff_tile), ff_tile)
            gate = jnp.dot(xbuf[used, :], wg[:, cols], preferred_element_type=jnp.float32)
            up = jnp.dot(xbuf[used, :], wu[:, cols], preferred_element_type=jnp.float32)
            act[used, cols] = (jax.nn.silu(gate) * up).astype(jnp.bfloat16)

        if is_first:
            loads[2].wait()

        @pl.loop(0, width // d_tile)
        def _(j):
            cols = pl.ds(pl.multiple_of(j * d_tile, d_tile), d_tile)
            xbuf[used, cols] = jnp.dot(
                act[used, :], wd[:, cols], preferred_element_type=jnp.float32
            ).astype(jnp.bfloat16)

        ret[got, :width] = xbuf[:count]
        across = lax.broadcasted_iota(jnp.int32, (count, extra), 1)
        down = lax.broadcasted_iota(jnp.int32, (count, extra), 0)
        spread = (across // REST) * BASE + across % REST
        back = jnp.zeros((count, PIECE), jnp.float32)
        for q, first, size in pieces(width):
            part = jnp.dot(
                onehot(spread + q * REST, down), xbuf[count : count + extra, first : first + size],
                preferred_element_type=jnp.float32,
            )
            if size < PIECE:
                part = jnp.concatenate(
                    [part, jnp.zeros((count, PIECE - size), jnp.float32)], axis=1
                )
            back = back + part
        ret[got, width:] = back.astype(jnp.bfloat16)

    for i, (begin, size) in enumerate(CHUNKS):
        low, high = begin * n // 16, (begin + size) * n // 16
        skip = 1 if low == half else 0

        @pl.loop(low + skip, high)
        def _(k):
            outward(k).wait_recv()

        work(low, high - low, i == 0)

        @pl.loop(low + skip, high)
        def _(k):
            homeward(k).start()

        if skip:
            out_ref[rows(me), :] = ret[pl.ds(half * BASE, BASE), :]

    @pl.loop(1, n)
    def _(t):
        d = (me + t) % n
        pltpu.make_async_remote_copy(
            src_ref=mod_own,
            dst_ref=mod_all.at[strip(d)],
            send_sem=mod_out_sem.at[0],
            recv_sem=mod_in_sem.at[d],
            device_id=(mine, d),
            device_id_type=MESH,
        ).wait_recv()

    stream = hidden_ref[...].astype(jnp.float32)
    centered = stream - jnp.mean(stream, axis=-1, keepdims=True)
    variance = jnp.mean(centered * centered, axis=-1, keepdims=True)
    normed = centered * lax.rsqrt(variance + 1e-06)
    modulation = jnp.concatenate([mod_all[d * 8 : d * 8 + 1, :piece] for d in range(n)], axis=1)
    shift = modulation[:, :width]
    scale = modulation[:, width : 2 * width]
    current = (normed * (1.0 + scale) + shift).astype(jnp.bfloat16)
    logits = lax.dot_general(
        router_ref[...], current, over_features, preferred_element_type=jnp.float32
    )
    picked = [jnp.sum(hot[k] * logits, axis=0, keepdims=True) for k in range(TOP)]
    weights = [
        jnp.broadcast_to(jax.nn.sigmoid(picked[k] - picked[1 - k]), (128, stream.shape[0])).T[:, :1]
        for k in range(TOP)
    ]
    row = lax.broadcasted_iota(jnp.int32, (n * BASE, stream.shape[0]), 0)
    table = (row // (BASE * group)) * BASE + row % BASE
    whole = [onehot(main[k], table) for k in range(TOP)]

    @pl.loop(1, n)
    def _(t):
        d = (me + t) % n
        pltpu.make_async_remote_copy(
            src_ref=ret.at[rows(0)],
            dst_ref=out_ref.at[rows(d)],
            send_sem=back_sem.at[0],
            recv_sem=home_sem.at[d],
            device_id=(mine, d),
            device_id_type=MESH,
        ).wait_recv()

    for q, first, size in pieces(width):
        cols = slice(first, first + size)
        routed = jnp.zeros((stream.shape[0], size), jnp.float32)
        for k in range(TOP):
            found = lax.dot_general(
                whole[k], out_ref[:, cols], over_rows, preferred_element_type=jnp.float32
            )
            found = found + lax.dot_general(
                onehot(rest[k] + q * REST, table), out_ref[:, width : width + size],
                over_rows, preferred_element_type=jnp.float32,
            )
            routed = routed + weights[k] * found
        gate = modulation[:, 2 * width + first : 2 * width + first + size]
        mixed_ref[:, cols] = (hidden_ref[:, cols].astype(jnp.float32) + gate * routed).astype(
            mixed_ref.dtype
        )

    for low, high in ((half // 2, half), (half + 1, n)):

        @pl.loop(low, high)
        def _(k):
            outward(k).wait_send()

    for low, high in ((0, half), (half + 1, n)):

        @pl.loop(low, high)
        def _(k):
            modward(k).wait_send()
            homeward(k).wait_send()


def local(
    hidden_now, stale_rows, expert_ids, condition, mod_weight, mod_bias, router, w_gate, w_up, w_down
):
    n = lax.axis_size("seq")
    width = hidden_now.shape[1]
    ff = w_gate.shape[1]
    ff_tile = 512 if ff % 512 == 0 else ff
    d_tile = 256
    message = width + PIECE
    per = max(size for _, size in CHUNKS) * n // 16
    piece = mod_bias.shape[0]
    lanes = -(-piece // 128) * 128
    vmem = pl.BlockSpec(memory_space=pltpu.VMEM)
    hbm = pl.BlockSpec(memory_space=pl.ANY)
    bf16 = jnp.bfloat16
    return pl.pallas_call(
        functools.partial(exchange, n, ff_tile, d_tile),
        out_shape=jax.ShapeDtypeStruct(hidden_now.shape, hidden_now.dtype),
        in_specs=[vmem] * 6 + [hbm] * 4,
        out_specs=vmem,
        scratch_shapes=[
            pltpu.VMEM(mod_weight.shape[::-1], bf16),
            pltpu.VMEM(w_gate.shape, bf16),
            pltpu.VMEM(w_up.shape, bf16),
            pltpu.VMEM(w_down.shape, bf16),
            pltpu.VMEM((EXPERTS * BASE, message), bf16),
            pltpu.VMEM((n * BASE, message), bf16),
            pltpu.VMEM((n * BASE, message), bf16),
            pltpu.VMEM((n * BASE, message), bf16),
            pltpu.VMEM((per * CAP, width), bf16),
            pltpu.VMEM((per * CAP, ff), bf16),
            pltpu.VMEM((8, lanes), jnp.float32),
            pltpu.VMEM((n * 8, lanes), jnp.float32),
            pltpu.SemaphoreType.DMA((4,)),
            pltpu.SemaphoreType.DMA((n,)),
            pltpu.SemaphoreType.DMA((n,)),
            pltpu.SemaphoreType.DMA((n,)),
            pltpu.SemaphoreType.DMA((n,)),
            pltpu.SemaphoreType.DMA((n,)),
            pltpu.SemaphoreType.DMA((n,)),
        ],
        compiler_params=pltpu.CompilerParams(
            collective_id=0, has_side_effects=True, vmem_limit_bytes=58 * 1024 * 1024
        ),
        cost_estimate=pl.CostEstimate(
            flops=6 * n * CAP * width * ff, bytes_accessed=6 * width * ff, transcendentals=0
        ),
        name="exchange",
    )(
        expert_ids.T, stale_rows, hidden_now, condition, mod_bias, router.T,
        mod_weight.T, w_gate, w_up, w_down,
    )


def solution(mesh):
    in_specs = (
        P(("groups", "seq"), None),
        P(("groups", "seq"), None),
        P(("groups", "seq"), None),
        P("groups"),
        P(None, "seq"),
        P("seq"),
        P(),
        P(None, "seq"),
        P(None, "seq"),
        P("seq", None),
    )
    out_specs = P(("groups", "seq"), None)
    return jax.shard_map(local, mesh=mesh, in_specs=in_specs, out_specs=out_specs, check_vma=False)
```
